1024 devices in a mesh: angle: 32 (over x_lo, y, core), scan: 32 (over z, x_hi).
Axes of the slice: x: 4 (x_hi: 2, x_lo: 2; x = x_hi * 2 + x_lo), y: 8, z: 16, core: 2. Of those that a mesh axis runs over, the one named last changes fastest.
Arguments:
- object_slices: float32 [2, 3, 2048, 512], P(None, None, 'scan', 'angle'), may hold values from -5 to 5
- probe: float32 [2, 128, 128], replicated, may hold values from -6 to 6
- intensities: float32 [32, 32, 2, 128, 128], P('angle', 'scan'), may hold values from 0.5 to 3.5
- row_offsets: int32 [32, 32, 2], P('angle', 'scan'), may hold values from 0 to 64
- column_starts: int32 [32, 32, 2], P('angle', 'scan'), may hold values from 0 to 320
- slice_shifts: int32 [32, 3], P('angle'), may hold values from 0 to 64
- counts: int32 [32, 32], P('angle', 'scan'), may hold values from 1 to 2, as said below
Outputs:
- object_gradient: float32 [2, 3, 2048, 512], P(None, None, 'scan', 'angle')
- probe_gradient: float32 [2, 128, 128], replicated
The draws below stay inside these ranges and needn't reach their ends.
Inputs may be any that keep to these rules, and one draw needn't show every extreme that they name: `counts`: the largest value 2 occurs in every draw.
All inputs are finite; a program needn't handle non-finite values.
Results may differ from the reference program's by a relative error of at most 0.0003.
Values sent between devices are 32-bit elements; how exact they have to be, the bound alone decides.
No kernel may reach another device: no remote copies, remote signals or barrier semaphores. Data moves between devices by JAX's collectives and lax.ppermute only.
A program may use at most 32 MiB of HBM per device.

```python
import jax
import jax.numpy as jnp
from jax import lax

PATCH = 128
LAYERS = 3
COLUMNS = 512
TILT = 64
BAND = 64
SLOTS = 2
ANGLES = 32
SCANS = 32
ROWS = 2048
N_ANGLE = 32
N_SCAN = 32


def draw_counts(key, part):
    first, second, third, fourth = jax.random.split(jax.random.fold_in(key, 17), 4)
    lefthand = jax.random.randint(first, (ANGLES, SCANS), 0, SLOTS)
    righthand = jax.random.randint(second, (ANGLES, SCANS), 0, SLOTS)
    values = SLOTS // 3 + 1 + lefthand * righthand // (2 * (SLOTS - 1))
    which_row = jax.random.randint(third, (), 0, ANGLES)
    which_column = jax.random.randint(fourth, (), 0, SCANS)
    return values.at[which_row, which_column].set(SLOTS).astype(jnp.int32)


def touch_ends(values, key, low, top_value):
    index_at = [jax.random.randint(jax.random.fold_in(key, axis), (), 0, length) for axis, length in enumerate(values.shape)]
    main_axis = values.shape.index(max(values.shape))
    next_to = index_at[:main_axis] + [(index_at[main_axis] + 1) % values.shape[main_axis]] + index_at[main_axis + 1:]
    return values.at[tuple(index_at)].set(low).at[tuple(next_to)].set(top_value)


def shard_levels(key, shape, cuts, least, high):
    gain = 1.0
    for axis_at, shards_of in cuts:
        steps = jax.random.uniform(jax.random.fold_in(jax.random.fold_in(key, 6), axis_at), (shards_of,), jnp.float32, least / len(cuts), high / len(cuts))
        gain = gain * jnp.repeat(jnp.exp(steps), shape[axis_at] // shards_of).reshape((-1,) + (1,) * (len(shape) - 1 - axis_at))
    return gain


def bell_draw(key, extent, spread, limit, pieces=(), kind=jnp.bfloat16):
    array = spread * jax.random.normal(key, extent, jnp.float32)
    if pieces:
        array = array * shard_levels(key, extent, pieces, -0.22, 0.18)
    return jnp.clip(array, -limit, limit).astype(kind)


def setup_inputs(seed: int = 0) -> dict:
    key_of = jax.random.split(jax.random.key(seed), 8)
    return {
        "object_slices": bell_draw(key_of[0], (2, LAYERS, ROWS, COLUMNS), 0.7, 5.0, ((2, 32), (3, 32)), jnp.float32),
        "probe": bell_draw(key_of[1], (2, PATCH, PATCH), 1.0, 6.0, (), jnp.float32),
        "intensities": jnp.clip(0.5 + 3.0 * jax.random.uniform(key_of[2], (ANGLES, SCANS, SLOTS, PATCH, PATCH), jnp.float32) ** shard_levels(key_of[2], (ANGLES, SCANS, SLOTS, PATCH, PATCH), ((0, 32), (1, 32)), -0.2, 0.2), 0.5, 3.5),
        "row_offsets": touch_ends(jax.random.randint(key_of[3], (ANGLES, SCANS, SLOTS), 0, 3 * BAND - PATCH + 1), jax.random.fold_in(key_of[3], 1), 0, 3 * BAND - PATCH).astype(jnp.int32),
        "column_starts": touch_ends(jax.random.randint(key_of[4], (ANGLES, SCANS, SLOTS), 0, COLUMNS - PATCH - TILT + 1), jax.random.fold_in(key_of[4], 1), 0, COLUMNS - PATCH - TILT).astype(jnp.int32),
        "slice_shifts": touch_ends(jax.random.randint(key_of[5], (ANGLES, LAYERS), 0, TILT + 1), jax.random.fold_in(key_of[5], 1), 0, TILT).astype(jnp.int32),
        "counts": draw_counts(jax.random.fold_in(key_of[7], 71), 0),
    }


def propagator(size):
    index = jnp.arange(size, dtype=jnp.int32)
    centred = ((index + size // 2) % size - size // 2).astype(jnp.float32)
    radius = centred[:, None] * centred[:, None] + centred[None, :] * centred[None, :]
    phase = 8.0 * jnp.pi * radius / (size * size)
    return (jnp.cos(phase), jnp.sin(phase))

def patch_loss(slab, probe, measured, weight):
    size = probe.shape[1]
    kern_re, kern_im = propagator(size)
    kernel = kern_re + 1j * kern_im
    wave = probe[0] + 1j * probe[1]
    layers = slab.shape[1]
    for k in range(layers):
        wave = wave * (slab[0, k] + 1j * slab[1, k])
        if k + 1 < layers:
            wave = jnp.fft.ifft2(kernel * jnp.fft.fft2(wave, norm='ortho'), norm='ortho')
    far = jnp.fft.fft2(wave, norm='ortho')
    power = jnp.real(far) * jnp.real(far) + jnp.imag(far) * jnp.imag(far)
    differ = power - measured
    return weight * jnp.sum(differ * differ)

def reference(object_slices, probe, intensities, row_offsets, column_starts, slice_shifts, counts):
    layers = object_slices.shape[1]
    rows = object_slices.shape[2]
    band = rows // N_SCAN
    size = probe.shape[1]
    slots = row_offsets.shape[2]
    padded = jnp.pad(object_slices, ((0, 0), (0, 0), (band, band), (0, 0)))
    total = N_ANGLE * N_SCAN * slots

    def visit(carry, index):
        gradient_object, gradient_probe = carry
        angle = index // (N_SCAN * slots)
        scanned = index // slots % N_SCAN
        slot = index % slots
        top = (scanned * band + row_offsets[angle, scanned, slot]).astype(jnp.int32)
        start = column_starts[angle, scanned, slot].astype(jnp.int32)
        shifts = slice_shifts[angle]
        zero = jnp.zeros((), jnp.int32)
        slab = jnp.concatenate([lax.dynamic_slice(padded, (zero, zero + k, top, start + shifts[k]), (2, 1, size, size)) for k in range(layers)], axis=1)
        weight = jnp.where(slot < counts[angle, scanned], 0.5 / N_ANGLE, 0.0).astype(jnp.float32)
        measured = intensities[angle, scanned, slot]
        loss, pull = jax.vjp(lambda s, p: patch_loss(s, p, measured, weight), slab, probe)
        slab_grad, probe_grad = pull(jnp.ones_like(loss))
        for k in range(layers):
            place = (zero, zero + k, top, start + shifts[k])
            current = lax.dynamic_slice(gradient_object, place, (2, 1, size, size))
            gradient_object = lax.dynamic_update_slice(gradient_object, current + slab_grad[:, k:k + 1], place)
        return ((gradient_object, gradient_probe + probe_grad), None)
    start_carry = (jnp.zeros(padded.shape, jnp.float32), jnp.zeros(probe.shape, jnp.float32))
    (gradient_object, gradient_probe), unused = lax.scan(visit, start_carry, jnp.arange(total, dtype=jnp.int32))
    return (gradient_object[:, :, band:band + rows], gradient_probe)
```

```python
import jax
import jax.numpy as jnp
import numpy as np
from jax import lax
from jax.experimental import pallas as pl
from jax.experimental.pallas import tpu as pltpu
from jax.sharding import Mesh
from jax.sharding import PartitionSpec as P

PLANE = ("xl", "y")
ANGLE = ("xl", "y", "c")
SCAN = ("z", "xh")
ANY = pl.BlockSpec(memory_space=pl.ANY)
VMEM = pl.BlockSpec(memory_space=pltpu.VMEM)
SMEM = pl.BlockSpec(memory_space=pltpu.SMEM)


def tables(size):
    index = np.arange(size)
    centred = ((index + size // 2) % size - size // 2).astype(np.float64)
    dft = np.exp(-2j * np.pi * (np.outer(index, index) % size) / size) / np.sqrt(size)
    step = dft.conj() @ (np.exp(8j * np.pi * centred * centred / size**2)[:, None] * dft)
    out = []
    for m in (0.5 * (step + step.T), dft):
        left = np.block([[m.real, -m.imag], [m.imag, m.real]])
        right = np.block([[m.real, m.imag], [-m.imag, m.real]])
        for block, axis in ((left, 1), (right, 0)):
            block = block.astype(np.float32)
            high = block.astype(jnp.bfloat16)
            low = (block - high.astype(np.float32)).astype(jnp.bfloat16)
            out.append(np.concatenate([high, low, high], axis=axis))
    return out


def parts(x, axis):
    high = x.astype(jnp.bfloat16)
    low = (x - high.astype(jnp.float32)).astype(jnp.bfloat16)
    return jnp.concatenate([high, high, low], axis=axis)


def two_sided(values, left, right):
    n = len(values)
    size = values[0][0].shape[0]
    stack = jnp.concatenate(
        [jnp.concatenate([v[i] for v in values], axis=1) for i in range(2)], axis=0
    )
    y = jnp.dot(left, parts(stack, 0), preferred_element_type=jnp.float32)
    rows = jnp.concatenate(
        [
            jnp.concatenate([y[i * size : (i + 1) * size, p * size : (p + 1) * size] for i in range(2)], axis=1)
            for p in range(n)
        ],
        axis=0,
    )
    z = jnp.dot(parts(rows, 1), right, preferred_element_type=jnp.float32)
    return [(z[p * size : (p + 1) * size, :size], z[p * size : (p + 1) * size, size:]) for p in range(n)]


def product(a, b):
    return (a[0] * b[0] - a[1] * b[1], a[0] * b[1] + a[1] * b[0])


def pack_kernel(own, before, after, out):
    layers, band = own.shape[1], own.shape[3]
    tiles = []
    for i in range(2):
        for k in range(layers):
            tiles.append(jnp.concatenate([before[i, k], own[i, k]], axis=1))
    for k in range(layers):
        tiles.append(jnp.concatenate([after[0, k], after[1, k]], axis=1))
    tile = jnp.stack(tiles)
    for q in range(out.shape[0]):
        out[q] = tile


def gradient_kernel(
    info, weights, probe, measured, step_l, step_r, dft_l, dft_r, mine, theirs,
    keep, send, keep_probe, send_probe, region, grown, sums, arrived, left_sem,
):
    slots, size = measured.shape[0], measured.shape[1]
    groups = region.shape[0]
    layers = groups // 3
    core = info[0]
    other = 1 - core
    copies = []
    for g in range(groups):
        copies.append(pltpu.make_async_copy(mine.at[:, g], region.at[g, :, core], arrived.at[2 * g]))
        copies.append(pltpu.make_async_copy(theirs.at[:, g], region.at[g, :, other], arrived.at[2 * g + 1]))
    for copy in copies:
        copy.start()
    grown[...] = jnp.zeros_like(grown)
    wave = (probe[0].T, probe[1].T)
    meas = [measured[p].T for p in range(slots)]
    for copy in copies:
        copy.wait()
    columns = region.shape[1] * region.shape[2] * region.shape[3]
    flat = region.reshape(groups, columns, size)
    grown_flat = grown.reshape(groups, columns, size)
    lane = lax.broadcasted_iota(jnp.int32, (size, size), 1)
    tops = [info[1 + p] for p in range(slots)]
    later = [lane < tops[p] for p in range(slots)]
    starts = [[info[1 + slots + p] + info[1 + 2 * slots + k] for k in range(layers)] for p in range(slots)]

    def window(p, k):
        at = pl.ds(starts[p][k], size)
        tail = flat[2 * layers + k, at]
        return (
            jnp.where(later[p], tail, flat[k, at]),
            jnp.where(later[p], pltpu.roll(tail, size // 2, 1), flat[layers + k, at]),
        )

    waves = [[tuple(pltpu.roll(w, tops[p], 1) for w in wave) for p in range(slots)]]
    for k in range(layers):
        leaving = [product(waves[k][p], window(p, k)) for p in range(slots)]
        if k + 1 < layers:
            waves.append(two_sided(leaving, step_l[...], step_r[...]))
        else:
            waves.append(two_sided(leaving, dft_l[...], dft_r[...]))
    back = []
    for p in range(slots):
        re, im = waves[layers][p]
        slope = (4.0 * weights[p]) * (re * re + im * im - meas[p])
        back.append((slope * re, -(slope * im)))
    for k in range(layers - 1, -1, -1):
        if k + 1 < layers:
            back = two_sided(back, step_l[...], step_r[...])
        else:
            back = two_sided(back, dft_l[...], dft_r[...])
        for p in range(slots):
            at = pl.ds(starts[p][k], size)
            re, im = product(waves[k][p], back[p])
            im = -im
            zero = jnp.zeros_like(re)
            grown_flat[k, at] += jnp.where(later[p], zero, re)
            grown_flat[layers + k, at] += jnp.where(later[p], zero, im)
            grown_flat[2 * layers + k, at] += jnp.where(later[p], re, zero) + pltpu.roll(
                jnp.where(later[p], im, zero), size // 2, 1
            )
        back = [product(window(p, k), back[p]) for p in range(slots)]
    total = []
    for i in range(2):
        total.append(
            sum(pltpu.roll(back[p][i], lax.rem(size - tops[p], size), 1) for p in range(slots))
        )
    pieces = (size // (8 * 2), 2, 8, size)
    sums[: pieces[0]] = total[0].T.reshape(pieces)
    sums[pieces[0] :] = (-total[1]).T.reshape(pieces)
    copies = [
        pltpu.make_async_copy(sums.at[:, core], keep_probe, left_sem.at[2 * groups]),
        pltpu.make_async_copy(sums.at[:, other], send_probe, left_sem.at[2 * groups + 1]),
    ]
    for g in range(groups):
        copies.append(pltpu.make_async_copy(grown.at[g, :, core], keep.at[:, g], left_sem.at[2 * g]))
        copies.append(pltpu.make_async_copy(grown.at[g, :, other], send.at[:, g], left_sem.at[2 * g + 1]))
    for copy in copies:
        copy.start()
    for copy in copies:
        copy.wait()


def spread(array, axes, count):
    return lax.all_to_all(jnp.broadcast_to(array[None], (count, *array.shape)), axes, 0, 0, tiled=True)


def local(object_slices, probe, intensities, row_offsets, column_starts, slice_shifts, counts):
    own = jnp.swapaxes(object_slices, 2, 3)
    layers, width, band = own.shape[1:]
    size = probe.shape[1]
    slots = row_offsets.shape[2]
    angles = lax.axis_size(ANGLE)
    plane = angles // 2
    scans = lax.axis_size(SCAN)
    up = [(i, i + 1) for i in range(scans - 1)]
    down = [(i + 1, i) for i in range(scans - 1)]
    swap = [(0, 1), (1, 0)]
    core = lax.axis_index("c")

    before = lax.ppermute(own, SCAN, up)
    after = lax.ppermute(own, SCAN, down)
    info = jnp.concatenate(
        [
            core.astype(jnp.int32)[None],
            row_offsets.reshape(slots),
            column_starts.reshape(slots),
            slice_shifts.reshape(layers),
        ]
    )
    weights = jnp.where(jnp.arange(slots) < counts[0, 0], 0.5 / angles, 0.0).astype(jnp.float32)
    groups = 3 * layers
    packed = pl.pallas_call(
        pack_kernel,
        out_shape=jax.ShapeDtypeStruct((plane, groups, width, 2 * band), jnp.float32),
        in_specs=[VMEM] * 3,
        out_specs=VMEM,
    )(own, before, after)
    mine = lax.all_to_all(packed, PLANE, 0, 0, tiled=True)
    theirs = lax.ppermute(mine, "c", swap)

    share = jax.ShapeDtypeStruct((plane, groups, width, size), jnp.float32)
    piece = jax.ShapeDtypeStruct((plane, 2 * size // angles, size), jnp.float32)
    keep, send, keep_probe, send_probe = pl.pallas_call(
        gradient_kernel,
        out_shape=(share, share, piece, piece),
        in_specs=[SMEM] * 2 + [VMEM] * 6 + [ANY] * 2,
        out_specs=[ANY] * 4,
        scratch_shapes=[
            pltpu.VMEM((groups, plane, 2, width, size), jnp.float32),
            pltpu.VMEM((groups, plane, 2, width, size), jnp.float32),
            pltpu.VMEM((plane, 2, 2 * size // angles, size), jnp.float32),
            pltpu.SemaphoreType.DMA((2 * groups,)),
            pltpu.SemaphoreType.DMA((2 * groups + 2,)),
        ],
        compiler_params=pltpu.CompilerParams(vmem_limit_bytes=40 * 1024 * 1024),
    )(info, weights, probe, intensities[0, 0], *[jnp.asarray(t) for t in tables(size)], mine, theirs)

    probe_part = keep_probe + lax.ppermute(send_probe, "c", swap)
    share_part = keep + lax.ppermute(send, "c", swap)
    probe_sum = lax.all_to_all(probe_part, PLANE, 0, 0, tiled=True).sum(axis=0)
    probe_sum = spread(probe_sum, SCAN, scans).sum(axis=0)
    probe_mine = spread(probe_sum, PLANE, plane)
    probe_theirs = lax.ppermute(probe_mine, "c", swap)
    probe_gradient = jnp.where(
        core == 0,
        jnp.stack([probe_mine, probe_theirs], axis=1),
        jnp.stack([probe_theirs, probe_mine], axis=1),
    ).reshape(probe.shape)

    share_sum = lax.all_to_all(share_part, PLANE, 0, 0, tiled=True).sum(axis=0)
    heads = share_sum[: 2 * layers].reshape(2, layers, width, size)
    from_after = lax.ppermute(heads[..., :band], SCAN, down)
    from_before = lax.ppermute(share_sum[2 * layers :], SCAN, up)
    object_gradient = (
        heads[..., band:] + from_after + jnp.stack([from_before[..., :band], from_before[..., band:]])
    )
    return (jnp.swapaxes(object_gradient, 2, 3), probe_gradient)


def solution(mesh):
    devices = mesh.devices.reshape(2, 8, 2, 16, 2)
    fine = Mesh(devices, ("xl", "y", "c", "z", "xh"))
    return jax.shard_map(
        local,
        mesh=fine,
        in_specs=(
            P(None, None, SCAN, ANGLE),
            P(),
            P(ANGLE, SCAN, None, None, None),
            P(ANGLE, SCAN, None),
            P(ANGLE, SCAN, None),
            P(ANGLE, None),
            P(ANGLE, SCAN),
        ),
        out_specs=(P(None, None, SCAN, ANGLE), P()),
        check_vma=False,
    )
```

```python
import jax
import jax.numpy as jnp
import numpy as np
from jax import lax
from jax.experimental import pallas as pl
from jax.experimental.pallas import tpu as pltpu
from jax.sharding import Mesh
from jax.sharding import PartitionSpec as P

PLANE = ("xl", "y")
ANGLE = ("xl", "y", "c")
SCAN = ("z", "xh")
ANY = pl.BlockSpec(memory_space=pl.ANY)
VMEM = pl.BlockSpec(memory_space=pltpu.VMEM)
SMEM = pl.BlockSpec(memory_space=pltpu.SMEM)
HBM = pl.BlockSpec(memory_space=pltpu.HBM)
SMALL = pltpu.CompilerParams(vmem_limit_bytes=8 * 1024 * 1024)


def tables(size):
    index = np.arange(size)
    centred = ((index + size // 2) % size - size // 2).astype(np.float64)
    dft = np.exp(-2j * np.pi * (np.outer(index, index) % size) / size) / np.sqrt(size)
    step = dft.conj() @ (np.exp(8j * np.pi * centred * centred / size**2)[:, None] * dft)
    whole = np.stack([np.stack([m.real, m.imag]) for m in (0.5 * (step + step.T), dft)]).astype(np.float32)
    high = whole.astype(jnp.bfloat16)
    low = (whole - high.astype(np.float32)).astype(jnp.bfloat16)
    return np.stack([high, low], axis=1)


def sides(table):
    left, right = [], []
    for part in (0, 1, 0):
        re, im = table[part, 0], table[part, 1]
        left.append(jnp.concatenate([jnp.concatenate([re, -im], axis=1), jnp.concatenate([im, re], axis=1)], axis=0))
        right.append(jnp.concatenate([jnp.concatenate([re, im], axis=1), jnp.concatenate([-im, re], axis=1)], axis=0))
    return jnp.concatenate(left, axis=1), jnp.concatenate(right, axis=0)


def parts(x, axis):
    high = x.astype(jnp.bfloat16)
    low = (x - high.astype(jnp.float32)).astype(jnp.bfloat16)
    return jnp.concatenate([high, high, low], axis=axis)


def two_sided(values, left, right):
    n = len(values)
    size = values[0][0].shape[0]
    stack = jnp.concatenate(
        [jnp.concatenate([v[i] for v in values], axis=1) for i in range(2)], axis=0
    )
    y = jnp.dot(left, parts(stack, 0), preferred_element_type=jnp.float32)
    rows = jnp.concatenate(
        [
            jnp.concatenate([y[i * size : (i + 1) * size, p * size : (p + 1) * size] for i in range(2)], axis=1)
            for p in range(n)
        ],
        axis=0,
    )
    z = jnp.dot(parts(rows, 1), right, preferred_element_type=jnp.float32)
    return [(z[p * size : (p + 1) * size, :size], z[p * size : (p + 1) * size, size:]) for p in range(n)]


def product(a, b):
    return (a[0] * b[0] - a[1] * b[1], a[0] * b[1] + a[1] * b[0])


def pack_kernel(own, out, many):
    tile = jnp.concatenate([own[0], own[1]], axis=2)
    out[...] = tile
    for q in range(many.shape[0]):
        many[q] = tile


def repeat_kernel(before, after, unused, many):
    layers = before.shape[0]
    for q in range(many.shape[0]):
        many[q, :layers] = before[...]
        many[q, layers:] = after[...]


def gradient_kernel(
    info, table, probe, measured, own_mine, own_theirs, rim_mine, rim_theirs,
    keep_near, keep_far, send_near, send_far, keep_probe, send_probe,
    region, grown, sums, table_here, probe_here, measured_here, arrived, left_sem,
):
    slots, size = measured.shape[0], measured.shape[1]
    groups = region.shape[0]
    layers = groups // 3
    half = size // 2
    rows = keep_near.shape[0]
    core = info[0]
    other = 1 - core
    near = info[1] * rows
    far = rows - near
    place = 2
    copies = []

    def fetch(source, target):
        copies.append(pltpu.make_async_copy(source, target, arrived.at[len(copies)]))

    fetch(table, table_here)
    fetch(probe, probe_here)
    fetch(measured, measured_here)
    for g in range(groups):
        mine, theirs, at = (own_mine, own_theirs, g) if g < layers else (rim_mine, rim_theirs, g - layers)
        fetch(mine.at[:, at], region.at[g, :, core])
        fetch(theirs.at[:, at], region.at[g, :, other])
    for copy in copies:
        copy.start()
    grown[...] = jnp.zeros_like(grown)
    for copy in copies:
        copy.wait()
    wave = (probe_here[0].T, probe_here[1].T)
    meas = [measured_here[p].T for p in range(slots)]
    step = sides(table_here[0])
    dft = sides(table_here[1])
    columns = region.shape[1] * region.shape[2] * region.shape[3]
    flat = region.reshape(groups, columns, size)
    grown_flat = grown.reshape(groups, columns, size)
    lane = lax.broadcasted_iota(jnp.int32, (size, size), 1)
    rim = lane < half
    folded = jnp.where(rim, lane, lane - half)
    tops = [info[place + p] for p in range(slots)]
    later = [folded < tops[p] for p in range(slots)]
    weights = [jnp.where(p < info[place + 2 * slots + layers], 4.0 * 0.5 / (4 * rows), 0.0) for p in range(slots)]
    starts = [
        [info[place + slots + p] + info[place + 2 * slots + k] for k in range(layers)] for p in range(slots)
    ]

    def window(p, k):
        at = pl.ds(starts[p][k], size)
        own = flat[k, at]
        ends = jnp.where(later[p], flat[2 * layers + k, at], flat[layers + k, at])
        return (
            jnp.where(rim, ends, pltpu.roll(own, half, 1)),
            jnp.where(rim, pltpu.roll(ends, half, 1), own),
        )

    waves = [[tuple(pltpu.roll(w, tops[p], 1) for w in wave) for p in range(slots)]]
    for k in range(layers):
        leaving = [product(waves[k][p], window(p, k)) for p in range(slots)]
        waves.append(two_sided(leaving, *(step if k + 1 < layers else dft)))
    back = []
    for p in range(slots):
        re, im = waves[layers][p]
        slope = weights[p] * (re * re + im * im - meas[p])
        back.append((slope * re, -(slope * im)))
    for k in range(layers - 1, -1, -1):
        back = two_sided(back, *(step if k + 1 < layers else dft))
        for p in range(slots):
            at = pl.ds(starts[p][k], size)
            re, im = product(waves[k][p], back[p])
            im = -im
            zero = jnp.zeros_like(re)
            ends = jnp.where(rim, re, pltpu.roll(im, half, 1))
            grown_flat[k, at] += jnp.where(rim, pltpu.roll(re, half, 1), im)
            grown_flat[layers + k, at] += jnp.where(later[p], zero, ends)
            grown_flat[2 * layers + k, at] += jnp.where(later[p], ends, zero)
        back = [product(window(p, k), back[p]) for p in range(slots)]
    total = []
    for i in range(2):
        total.append(sum(pltpu.roll(back[p][i], lax.rem(size - tops[p], size), 1) for p in range(slots)))
    pieces = (size // (8 * 2), 2, 8, size)
    sums[: pieces[0]] = total[0].T.reshape(pieces)
    sums[pieces[0] :] = (-total[1]).T.reshape(pieces)
    copies = []

    def leave(source, target):
        copies.append(pltpu.make_async_copy(source, target, left_sem.at[len(copies)]))

    leave(sums.at[:, core], keep_probe)
    leave(sums.at[:, other], send_probe)
    for g in range(groups):
        leave(grown.at[g, pl.ds(near, rows), core], keep_near.at[:, g])
        leave(grown.at[g, pl.ds(far, rows), core], keep_far.at[:, g])
        leave(grown.at[g, pl.ds(near, rows), other], send_near.at[:, g])
        leave(grown.at[g, pl.ds(far, rows), other], send_far.at[:, g])
    for copy in copies:
        copy.start()
    for copy in copies:
        copy.wait()


def scatter_sum_kernel(parts, many):
    total = parts[0]
    for q in range(1, parts.shape[0]):
        total = total + parts[q]
    for q in range(many.shape[0]):
        many[q] = total


def finish_kernel(shares, parts, own, before, after, many):
    layers = own.shape[0]
    for first, out in ((0, own), (layers, before), (2 * layers, after)):
        total = shares[0, first : first + layers]
        for q in range(1, shares.shape[0]):
            total = total + shares[q, first : first + layers]
        out[...] = total
    scatter_sum_kernel(parts, many)


def close_kernel(own, from_after, from_before, probe_mine, out, probe_out):
    probe_out[...] = probe_mine[...]
    half = own.shape[2] // 2
    total = own[...] + from_after[...] + from_before[...]
    out[0] = total[:, :, :half]
    out[1] = total[:, :, half:]


def merge_kernel(info, mine, theirs, out):
    core = info[0]
    out[:, core] = mine[...]
    out[:, 1 - core] = theirs[...]


def exchanged(array, axes):
    return lax.all_to_all(array, axes, 0, 0, tiled=True)


def local(object_slices, probe, intensities, row_offsets, column_starts, slice_shifts, counts):
    own = jnp.swapaxes(object_slices, 2, 3)
    layers, width, band = own.shape[1:]
    size = probe.shape[1]
    slots = row_offsets.shape[2]
    angles = lax.axis_size(ANGLE)
    plane = angles // 2
    rows = plane // 2
    scans = lax.axis_size(SCAN)
    up = [(i, i + 1) for i in range(scans - 1)]
    down = [(i + 1, i) for i in range(scans - 1)]
    swap = [(0, 1), (1, 0)]
    core = lax.axis_index("c")
    tile = (layers, width, 2 * band)
    groups = 3 * layers
    info = jnp.concatenate(
        [
            core.astype(jnp.int32)[None],
            lax.axis_index("xl").astype(jnp.int32)[None],
            row_offsets.reshape(slots),
            column_starts.reshape(slots),
            slice_shifts.reshape(layers),
            counts.reshape(1),
        ]
    )

    packed, packed_many = pl.pallas_call(
        pack_kernel,
        out_shape=(
            jax.ShapeDtypeStruct(tile, jnp.float32),
            jax.ShapeDtypeStruct((plane, *tile), jnp.float32),
        ),
        in_specs=[VMEM],
        out_specs=(VMEM, VMEM),
        compiler_params=SMALL,
    )(own)
    own_mine = exchanged(packed_many, PLANE)
    before = lax.ppermute(packed, SCAN, up)
    after = lax.ppermute(packed, SCAN, down)
    rim_many = pl.pallas_call(
        repeat_kernel,
        out_shape=jax.ShapeDtypeStruct((plane, 2 * layers, *tile[1:]), jnp.float32),
        in_specs=[VMEM] * 2 + [ANY],
        out_specs=VMEM,
        compiler_params=SMALL,
    )(before, after, own_mine)
    own_theirs = lax.ppermute(own_mine, "c", swap)
    rim_mine = exchanged(rim_many, PLANE)
    rim_theirs = lax.ppermute(rim_mine, "c", swap)

    share = jax.ShapeDtypeStruct((rows, groups, width, size), jnp.float32)
    piece = jax.ShapeDtypeStruct((plane, 2 * size // angles, size), jnp.float32)
    table = jnp.asarray(tables(size))
    keep_near, keep_far, send_near, send_far, keep_probe, send_probe = pl.pallas_call(
        gradient_kernel,
        out_shape=(share, share, share, share, piece, piece),
        in_specs=[SMEM] + [HBM] * 3 + [ANY] * 4,
        out_specs=[ANY] * 6,
        scratch_shapes=[
            pltpu.VMEM((groups, plane, 2, width, size), jnp.float32),
            pltpu.VMEM((groups, plane, 2, width, size), jnp.float32),
            pltpu.VMEM((plane, 2, 2 * size // angles, size), jnp.float32),
            pltpu.VMEM(table.shape, jnp.bfloat16),
            pltpu.VMEM(probe.shape, jnp.float32),
            pltpu.VMEM((slots, size, size), jnp.float32),
            pltpu.SemaphoreType.DMA((2 * groups + 3,)),
            pltpu.SemaphoreType.DMA((4 * groups + 2,)),
        ],
        compiler_params=pltpu.CompilerParams(vmem_limit_bytes=32 * 1024 * 1024),
    )(info, table, probe, intensities[0, 0], own_mine, own_theirs, rim_mine, rim_theirs)

    probe_part = keep_probe + lax.ppermute(send_probe, "c", swap)
    probe_part, send_far, send_near = lax.optimization_barrier((probe_part, send_far, send_near))
    bit = probe_part.shape[1:]
    probe_many = pl.pallas_call(
        scatter_sum_kernel,
        out_shape=jax.ShapeDtypeStruct((scans, *bit), jnp.float32),
        in_specs=[VMEM],
        out_specs=VMEM,
        compiler_params=SMALL,
    )(exchanged(probe_part, PLANE))
    probe_many = exchanged(probe_many, SCAN)

    part_far = keep_far + lax.ppermute(send_far, "c", swap)
    part_near = keep_near + lax.ppermute(send_near, "c", swap)
    part = part_near + lax.ppermute(part_far, "xl", swap)
    tile_out = jax.ShapeDtypeStruct(tile, jnp.float32)
    own_sum, to_before, to_after, probe_many = pl.pallas_call(
        finish_kernel,
        out_shape=(tile_out, tile_out, tile_out, jax.ShapeDtypeStruct((plane, *bit), jnp.float32)),
        in_specs=[VMEM] * 2,
        out_specs=[VMEM] * 4,
        compiler_params=SMALL,
    )(exchanged(part, "y"), probe_many)

    probe_mine = exchanged(probe_many, PLANE)
    from_after = lax.ppermute(to_before, SCAN, down)
    from_before = lax.ppermute(to_after, SCAN, up)
    object_gradient, probe_mine = pl.pallas_call(
        close_kernel,
        out_shape=(
            jax.ShapeDtypeStruct(own.shape, jnp.float32),
            jax.ShapeDtypeStruct(probe_mine.shape, jnp.float32),
        ),
        in_specs=[VMEM] * 4,
        out_specs=(VMEM, VMEM),
        compiler_params=SMALL,
    )(own_sum, from_after, from_before, probe_mine)
    probe_theirs = lax.ppermute(probe_mine, "c", swap)
    probe_gradient = pl.pallas_call(
        merge_kernel,
        out_shape=jax.ShapeDtypeStruct((plane, 2, *bit), jnp.float32),
        in_specs=[SMEM, VMEM, VMEM],
        out_specs=VMEM,
        compiler_params=SMALL,
    )(info, probe_mine, probe_theirs).reshape(probe.shape)
    return (jnp.swapaxes(object_gradient, 2, 3), probe_gradient)


def solution(mesh):
    devices = mesh.devices.reshape(2, 8, 2, 16, 2)
    fine = Mesh(devices, ("xl", "y", "c", "z", "xh"))
    return jax.shard_map(
        local,
        mesh=fine,
        in_specs=(
            P(None, None, SCAN, ANGLE),
            P(),
            P(ANGLE, SCAN, None, None, None),
            P(ANGLE, SCAN, None),
            P(ANGLE, SCAN, None),
            P(ANGLE, None),
            P(ANGLE, SCAN),
        ),
        out_specs=(P(None, None, SCAN, ANGLE), P()),
        check_vma=False,
    )
```

```python
import jax
import jax.numpy as jnp
import numpy as np
from jax import lax
from jax.experimental import pallas as pl
from jax.experimental.pallas import tpu as pltpu
from jax.sharding import Mesh
from jax.sharding import PartitionSpec as P

PLANE = ("xl", "y")
ANGLE = ("xl", "y", "c")
SCAN = ("z", "xh")
ROW = ("xl", "c", "xh")
ANY = pl.BlockSpec(memory_space=pl.ANY)
VMEM = pl.BlockSpec(memory_space=pltpu.VMEM)
SMEM = pl.BlockSpec(memory_space=pltpu.SMEM)
HBM = pl.BlockSpec(memory_space=pltpu.HBM)
URGENT = pl.CostEstimate(flops=50_000_000_000, bytes_accessed=1_000_000, transcendentals=0)
SMALL = pltpu.CompilerParams(vmem_limit_bytes=8 * 1024 * 1024)


def tables(size):
    index = np.arange(size)
    centred = ((index + size // 2) % size - size // 2).astype(np.float64)
    dft = np.exp(-2j * np.pi * (np.outer(index, index) % size) / size) / np.sqrt(size)
    step = dft.conj() @ (np.exp(8j * np.pi * centred * centred / size**2)[:, None] * dft)
    whole = np.stack([np.stack([m.real, m.imag]) for m in (0.5 * (step + step.T), dft)]).astype(np.float32)
    high = whole.astype(jnp.bfloat16)
    low = (whole - high.astype(np.float32)).astype(jnp.bfloat16)
    return np.stack([high, low], axis=1)


def sides(table):
    left, right = [], []
    for part in (0, 1, 0):
        re, im = table[part, 0], table[part, 1]
        left.append(jnp.concatenate([jnp.concatenate([re, -im], axis=1), jnp.concatenate([im, re], axis=1)], axis=0))
        right.append(jnp.concatenate([jnp.concatenate([re, im], axis=1), jnp.concatenate([-im, re], axis=1)], axis=0))
    return jnp.concatenate(left, axis=1), jnp.concatenate(right, axis=0)


def parts(x, axis):
    high = x.astype(jnp.bfloat16)
    low = (x - high.astype(jnp.float32)).astype(jnp.bfloat16)
    return jnp.concatenate([high, high, low], axis=axis)


def two_sided(values, left, right):
    n = len(values)
    size = values[0][0].shape[0]
    stack = jnp.concatenate(
        [jnp.concatenate([v[i] for v in values], axis=1) for i in range(2)], axis=0
    )
    y = jnp.dot(left, parts(stack, 0), preferred_element_type=jnp.float32)
    rows = jnp.concatenate(
        [
            jnp.concatenate([y[i * size : (i + 1) * size, p * size : (p + 1) * size] for i in range(2)], axis=1)
            for p in range(n)
        ],
        axis=0,
    )
    z = jnp.dot(parts(rows, 1), right, preferred_element_type=jnp.float32)
    return [(z[p * size : (p + 1) * size, :size], z[p * size : (p + 1) * size, size:]) for p in range(n)]


def product(a, b):
    return (a[0] * b[0] - a[1] * b[1], a[0] * b[1] + a[1] * b[0])


def pack_kernel(own, out, many):
    tile = jnp.concatenate([own[0], own[1]], axis=2)
    out[...] = tile
    for q in range(many.shape[0]):
        many[q] = tile


def repeat_kernel(info, paired, crossed, unused, many):
    layers = paired.shape[0]
    odd = info[0] == 1
    before = jnp.where(odd, paired[...], crossed[...])
    after = jnp.where(odd, crossed[...], paired[...])
    for q in range(many.shape[0]):
        many[q, :layers] = before
        many[q, layers:] = after


def gradient_kernel(
    info, table, probe, measured, own_mine, own_theirs, rim_mine, rim_theirs,
    keep_near, keep_far, send_near, send_far, probe_sums,
    region, grown, sums, table_here, probe_here, measured_here, arrived, left_sem,
):
    slots, size = measured.shape[0], measured.shape[1]
    groups = region.shape[0]
    layers = groups // 3
    half = size // 2
    rows = keep_near.shape[0]
    core = info[0]
    other = 1 - core
    near = info[1] * rows
    far = rows - near
    place = 2
    copies = []

    def fetch(source, target):
        copies.append(pltpu.make_async_copy(source, target, arrived.at[len(copies)]))

    fetch(table, table_here)
    fetch(probe, probe_here)
    fetch(measured, measured_here)
    for g in range(groups):
        mine, theirs, at = (own_mine, own_theirs, g) if g < layers else (rim_mine, rim_theirs, g - layers)
        fetch(mine.at[:, at], region.at[g, :, core])
        fetch(theirs.at[:, at], region.at[g, :, other])
    for copy in copies:
        copy.start()
    grown[...] = jnp.zeros_like(grown)
    for copy in copies:
        copy.wait()
    wave = (probe_here[0].T, probe_here[1].T)
    meas = [measured_here[p].T for p in range(slots)]
    step = sides(table_here[0])
    dft = sides(table_here[1])
    columns = region.shape[1] * region.shape[2] * region.shape[3]
    flat = region.reshape(groups, columns, size)
    grown_flat = grown.reshape(groups, columns, size)
    lane = lax.broadcasted_iota(jnp.int32, (size, size), 1)
    rim = lane < half
    folded = jnp.where(rim, lane, lane - half)
    tops = [info[place + p] for p in range(slots)]
    later = [folded < tops[p] for p in range(slots)]
    weights = [jnp.where(p < info[place + 2 * slots + layers], 4.0 * 0.5 / (4 * rows), 0.0) for p in range(slots)]
    starts = [
        [info[place + slots + p] + info[place + 2 * slots + k] for k in range(layers)] for p in range(slots)
    ]

    def window(p, k):
        at = pl.ds(starts[p][k], size)
        own = flat[k, at]
        ends = jnp.where(later[p], flat[2 * layers + k, at], flat[layers + k, at])
        return (
            jnp.where(rim, ends, pltpu.roll(own, half, 1)),
            jnp.where(rim, pltpu.roll(ends, half, 1), own),
        )

    waves = [[tuple(pltpu.roll(w, tops[p], 1) for w in wave) for p in range(slots)]]
    for k in range(layers):
        leaving = [product(waves[k][p], window(p, k)) for p in range(slots)]
        waves.append(two_sided(leaving, *(step if k + 1 < layers else dft)))
    back = []
    for p in range(slots):
        re, im = waves[layers][p]
        slope = weights[p] * (re * re + im * im - meas[p])
        back.append((slope * re, -(slope * im)))
    for k in range(layers - 1, -1, -1):
        back = two_sided(back, *(step if k + 1 < layers else dft))
        for p in range(slots):
            at = pl.ds(starts[p][k], size)
            re, im = product(waves[k][p], back[p])
            im = -im
            zero = jnp.zeros_like(re)
            ends = jnp.where(rim, re, pltpu.roll(im, half, 1))
            grown_flat[k, at] += jnp.where(rim, pltpu.roll(re, half, 1), im)
            grown_flat[layers + k, at] += jnp.where(later[p], zero, ends)
            grown_flat[2 * layers + k, at] += jnp.where(later[p], ends, zero)
        back = [product(window(p, k), back[p]) for p in range(slots)]
    total = []
    for i in range(2):
        total.append(sum(pltpu.roll(back[p][i], lax.rem(size - tops[p], size), 1) for p in range(slots)))
    pieces = sums.shape[0] // 2
    sums[:pieces] = total[0].T.reshape(pieces, *sums.shape[1:])
    sums[pieces:] = (-total[1]).T.reshape(pieces, *sums.shape[1:])
    copies = []

    def leave(source, target):
        copies.append(pltpu.make_async_copy(source, target, left_sem.at[len(copies)]))

    leave(sums, probe_sums)
    for g in range(groups):
        leave(grown.at[g, pl.ds(near, rows), core], keep_near.at[:, g])
        leave(grown.at[g, pl.ds(far, rows), core], keep_far.at[:, g])
        leave(grown.at[g, pl.ds(near, rows), other], send_near.at[:, g])
        leave(grown.at[g, pl.ds(far, rows), other], send_far.at[:, g])
    for copy in copies:
        copy.start()
    for copy in copies:
        copy.wait()


def summed(parts, first, last):
    total = parts[0, first:last]
    for q in range(1, parts.shape[0]):
        total = total + parts[q, first:last]
    return total


def probe_kernel(parts, many):
    total = summed(parts, 0, parts.shape[1])
    for q in range(many.shape[0]):
        many[q] = total


def share_kernel(info, kept, swapped, crossed, own, to_paired, to_crossed):
    layers = own.shape[1]
    odd = info[0] == 1
    for q in range(own.shape[0]):
        total = kept[q] + swapped[q] + crossed[q]
        before, after = total[layers : 2 * layers], total[2 * layers :]
        own[q] = total[:layers]
        to_paired[q] = jnp.where(odd, before, after)
        to_crossed[q] = jnp.where(odd, after, before)


def join_kernel(own, from_paired, from_crossed, parts, out):
    layers = own.shape[1]
    total = summed(parts, 0, parts.shape[1])
    total = total.reshape(out.shape[1] - layers, *out.shape[2:])
    for q in range(out.shape[0]):
        out[q, :layers] = own[q] + from_paired[q] + from_crossed[q]
        out[q, layers:] = total


def finish_kernel(shares, object_out, probe_out):
    layers, half = object_out.shape[1], object_out.shape[3]
    total = summed(shares, 0, layers)
    object_out[0] = total[:, :, :half]
    object_out[1] = total[:, :, half:]
    for q in range(shares.shape[0]):
        probe_out[q] = shares[q, layers:].reshape(probe_out.shape[1:])


def exchanged(array, axes):
    return lax.all_to_all(array, axes, 0, 0, tiled=True)


def local(object_slices, probe, intensities, row_offsets, column_starts, slice_shifts, counts):
    own = jnp.swapaxes(object_slices, 2, 3)
    layers, width, band = own.shape[1:]
    size = probe.shape[1]
    slots = row_offsets.shape[2]
    angles = lax.axis_size(ANGLE)
    plane = angles // 2
    rows = plane // 2
    scans = lax.axis_size(SCAN)
    pairs = [(i, i ^ 1) for i in range(scans)]
    others = [(i, i + 1 if i % 2 else i - 1) for i in range(1, scans - 1)]
    odd = lax.axis_index("xh").astype(jnp.int32)[None]
    swap = [(0, 1), (1, 0)]
    core = lax.axis_index("c")
    tile = (layers, width, 2 * band)
    groups = 3 * layers
    info = jnp.concatenate(
        [
            core.astype(jnp.int32)[None],
            lax.axis_index("xl").astype(jnp.int32)[None],
            row_offsets.reshape(slots),
            column_starts.reshape(slots),
            slice_shifts.reshape(layers),
            counts.reshape(1),
        ]
    )

    packed, packed_many = pl.pallas_call(
        pack_kernel,
        out_shape=(
            jax.ShapeDtypeStruct(tile, jnp.float32),
            jax.ShapeDtypeStruct((plane, *tile), jnp.float32),
        ),
        in_specs=[VMEM],
        out_specs=(VMEM, VMEM),
        compiler_params=SMALL,
    )(own)
    own_mine = exchanged(packed_many, PLANE)
    paired = lax.ppermute(packed, SCAN, pairs)
    crossed = lax.ppermute(packed, SCAN, others)
    rim_many = pl.pallas_call(
        repeat_kernel,
        out_shape=jax.ShapeDtypeStruct((plane, 2 * layers, *tile[1:]), jnp.float32),
        in_specs=[SMEM] + [VMEM] * 2 + [ANY],
        out_specs=VMEM,
        compiler_params=SMALL,
    )(odd, paired, crossed, own_mine)
    own_theirs = lax.ppermute(own_mine, "c", swap)
    rim_mine = exchanged(rim_many, PLANE)
    rim_theirs = lax.ppermute(rim_mine, "c", swap)

    share = jax.ShapeDtypeStruct((rows, groups, width, size), jnp.float32)
    depth = lax.axis_size("z")
    piece = jax.ShapeDtypeStruct((rows, 2 * size // rows, size), jnp.float32)
    table = jnp.asarray(tables(size))
    keep_near, keep_far, send_near, send_far, probe_sums = pl.pallas_call(
        gradient_kernel,
        out_shape=(share, share, share, share, piece),
        in_specs=[SMEM] + [HBM] * 3 + [ANY] * 4,
        out_specs=[HBM] * 5,
        scratch_shapes=[
            pltpu.VMEM((groups, plane, 2, width, size), jnp.float32),
            pltpu.VMEM((groups, plane, 2, width, size), jnp.float32),
            pltpu.VMEM(piece.shape, jnp.float32),
            pltpu.VMEM(table.shape, jnp.bfloat16),
            pltpu.VMEM(probe.shape, jnp.float32),
            pltpu.VMEM((slots, size, size), jnp.float32),
            pltpu.SemaphoreType.DMA((2 * groups + 3,)),
            pltpu.SemaphoreType.DMA((4 * groups + 1,)),
        ],
        compiler_params=pltpu.CompilerParams(vmem_limit_bytes=52 * 1024 * 1024),
    )(info, table, probe, intensities[0, 0], own_mine, own_theirs, rim_mine, rim_theirs)

    def probe_total(parts, count):
        return pl.pallas_call(
            probe_kernel,
            out_shape=jax.ShapeDtypeStruct((count, *piece.shape[1:]), jnp.float32),
            in_specs=[VMEM],
            out_specs=VMEM,
            compiler_params=SMALL,
            cost_estimate=URGENT,
        )(parts)

    parts = exchanged(probe_sums, "y")
    parts = exchanged(probe_total(parts, depth), "z")
    parts = exchanged(probe_total(parts, lax.axis_size(ROW)), ROW)

    part_far = keep_far + lax.ppermute(send_far, "c", swap)
    swapped = lax.ppermute(send_near, "c", swap)
    crossed = lax.ppermute(part_far, "xl", swap)
    band_share = jax.ShapeDtypeStruct((rows, *tile), jnp.float32)
    own_share, to_paired, to_crossed = pl.pallas_call(
        share_kernel,
        out_shape=(band_share, band_share, band_share),
        in_specs=[SMEM] + [VMEM] * 3,
        out_specs=[VMEM] * 3,
        compiler_params=SMALL,
    )(odd, keep_near, swapped, crossed)
    from_paired = lax.ppermute(to_paired, SCAN, pairs)
    from_crossed = lax.ppermute(to_crossed, SCAN, others)
    extra = piece.shape[1] // width
    joined = pl.pallas_call(
        join_kernel,
        out_shape=jax.ShapeDtypeStruct((rows, layers + extra, width, size), jnp.float32),
        in_specs=[VMEM] * 4,
        out_specs=VMEM,
        compiler_params=SMALL,
    )(own_share, from_paired, from_crossed, parts)
    object_gradient, probe_gradient = pl.pallas_call(
        finish_kernel,
        out_shape=(jax.ShapeDtypeStruct(own.shape, jnp.float32), piece),
        in_specs=[VMEM],
        out_specs=[VMEM] * 2,
        compiler_params=SMALL,
    )(exchanged(joined, "y"))
    return (jnp.swapaxes(object_gradient, 2, 3), probe_gradient.reshape(probe.shape))


def solution(mesh):
    devices = mesh.devices.reshape(2, 8, 2, 16, 2)
    fine = Mesh(devices, ("xl", "y", "c", "z", "xh"))
    return jax.shard_map(
        local,
        mesh=fine,
        in_specs=(
            P(None, None, SCAN, ANGLE),
            P(),
            P(ANGLE, SCAN, None, None, None),
            P(ANGLE, SCAN, None),
            P(ANGLE, SCAN, None),
            P(ANGLE, None),
            P(ANGLE, SCAN),
        ),
        out_specs=(P(None, None, SCAN, ANGLE), P()),
        check_vma=False,
    )
```

```python
import jax
import jax.numpy as jnp
import numpy as np
from jax import lax
from jax.experimental import pallas as pl
from jax.experimental.pallas import tpu as pltpu
from jax.sharding import Mesh
from jax.sharding import PartitionSpec as P

PLANE = ("xl", "y")
ANGLE = ("xl", "y", "c")
SCAN = ("z", "xh")
ROW = ("xl", "c", "xh")
ANY = pl.BlockSpec(memory_space=pl.ANY)
VMEM = pl.BlockSpec(memory_space=pltpu.VMEM)
SMEM = pl.BlockSpec(memory_space=pltpu.SMEM)
HBM = pl.BlockSpec(memory_space=pltpu.HBM)
URGENT = pl.CostEstimate(flops=50_000_000_000, bytes_accessed=1_000_000, transcendentals=0)
SMALL = pltpu.CompilerParams(vmem_limit_bytes=8 * 1024 * 1024)


def tables(size):
    index = np.arange(size)
    centred = ((index + size // 2) % size - size // 2).astype(np.float64)
    dft = np.exp(-2j * np.pi * (np.outer(index, index) % size) / size) / np.sqrt(size)
    step = dft.conj() @ (np.exp(8j * np.pi * centred * centred / size**2)[:, None] * dft)
    whole = np.stack([np.stack([m.real, m.imag]) for m in (0.5 * (step + step.T), dft)]).astype(np.float32)
    high = whole.astype(jnp.bfloat16)
    low = (whole - high.astype(np.float32)).astype(jnp.bfloat16)
    return np.stack([high, low], axis=1)


def sides(table):
    left, right = [], []
    for part in (0, 1, 0):
        re, im = table[part, 0], table[part, 1]
        left.append(jnp.concatenate([jnp.concatenate([re, -im], axis=1), jnp.concatenate([im, re], axis=1)], axis=0))
        right.append(jnp.concatenate([jnp.concatenate([re, im], axis=1), jnp.concatenate([-im, re], axis=1)], axis=0))
    return jnp.concatenate(left, axis=1), jnp.concatenate(right, axis=0)


def parts(x, axis):
    high = x.astype(jnp.bfloat16)
    low = (x - high.astype(jnp.float32)).astype(jnp.bfloat16)
    return jnp.concatenate([high, high, low], axis=axis)


def two_sided(values, left, right):
    n = len(values)
    size = values[0][0].shape[0]
    stack = jnp.concatenate(
        [jnp.concatenate([v[i] for v in values], axis=1) for i in range(2)], axis=0
    )
    y = jnp.dot(left, parts(stack, 0), preferred_element_type=jnp.float32)
    rows = jnp.concatenate(
        [
            jnp.concatenate([y[i * size : (i + 1) * size, p * size : (p + 1) * size] for i in range(2)], axis=1)
            for p in range(n)
        ],
        axis=0,
    )
    z = jnp.dot(parts(rows, 1), right, preferred_element_type=jnp.float32)
    return [(z[p * size : (p + 1) * size, :size], z[p * size : (p + 1) * size, size:]) for p in range(n)]


def product(a, b):
    return (a[0] * b[0] - a[1] * b[1], a[0] * b[1] + a[1] * b[0])


def pack_kernel(own, out, many):
    tile = jnp.concatenate([own[0], own[1]], axis=2)
    out[...] = tile
    for q in range(many.shape[0]):
        many[q] = tile


def repeat_kernel(info, paired, crossed, unused, many):
    layers = paired.shape[0]
    odd = info[0] == 1
    before = jnp.where(odd, paired[...], crossed[...])
    after = jnp.where(odd, crossed[...], paired[...])
    for q in range(many.shape[0]):
        many[q, :layers] = before
        many[q, layers:] = after


def gradient_kernel(
    info, table, probe, measured, own_mine, own_theirs, rim_mine, rim_theirs,
    keep_near, keep_far, send_near, send_far, probe_sums,
    region, grown, sums, table_here, probe_here, measured_here, arrived, left_sem,
):
    slots, size = measured.shape[0], measured.shape[1]
    groups = region.shape[0]
    layers = groups // 3
    half = size // 2
    rows = keep_near.shape[0]
    core = info[0]
    other = 1 - core
    near = info[1] * rows
    far = rows - near
    place = 2
    copies = []

    def fetch(source, target):
        copies.append(pltpu.make_async_copy(source, target, arrived.at[len(copies)]))

    fetch(table, table_here)
    fetch(probe, probe_here)
    fetch(measured, measured_here)
    for g in range(groups):
        mine, theirs, at = (own_mine, own_theirs, g) if g < layers else (rim_mine, rim_theirs, g - layers)
        fetch(mine.at[:, at], region.at[g, :, core])
        fetch(theirs.at[:, at], region.at[g, :, other])
    for copy in copies:
        copy.start()
    grown[...] = jnp.zeros_like(grown)
    for copy in copies:
        copy.wait()
    wave = (probe_here[0].T, probe_here[1].T)
    meas = [measured_here[p].T for p in range(slots)]
    step = sides(table_here[0])
    dft = sides(table_here[1])
    columns = region.shape[1] * region.shape[2] * region.shape[3]
    flat = region.reshape(groups, columns, size)
    grown_flat = grown.reshape(groups, columns, size)
    lane = lax.broadcasted_iota(jnp.int32, (size, size), 1)
    rim = lane < half
    folded = jnp.where(rim, lane, lane - half)
    tops = [info[place + p] for p in range(slots)]
    later = [folded < tops[p] for p in range(slots)]
    weights = [jnp.where(p < info[place + 2 * slots + layers], 4.0 * 0.5 / (4 * rows), 0.0) for p in range(slots)]
    starts = [
        [info[place + slots + p] + info[place + 2 * slots + k] for k in range(layers)] for p in range(slots)
    ]

    def window(p, k):
        at = pl.ds(starts[p][k], size)
        own = flat[k, at]
        ends = jnp.where(later[p], flat[2 * layers + k, at], flat[layers + k, at])
        return (
            jnp.where(rim, ends, pltpu.roll(own, half, 1)),
            jnp.where(rim, pltpu.roll(ends, half, 1), own),
        )

    waves = [[tuple(pltpu.roll(w, tops[p], 1) for w in wave) for p in range(slots)]]
    for k in range(layers):
        leaving = [product(waves[k][p], window(p, k)) for p in range(slots)]
        waves.append(two_sided(leaving, *(step if k + 1 < layers else dft)))
    back = []
    for p in range(slots):
        re, im = waves[layers][p]
        slope = weights[p] * (re * re + im * im - meas[p])
        back.append((slope * re, -(slope * im)))
    for k in range(layers - 1, -1, -1):
        back = two_sided(back, *(step if k + 1 < layers else dft))
        for p in range(slots):
            at = pl.ds(starts[p][k], size)
            re, im = product(waves[k][p], back[p])
            im = -im
            zero = jnp.zeros_like(re)
            ends = jnp.where(rim, re, pltpu.roll(im, half, 1))
            grown_flat[k, at] += jnp.where(rim, pltpu.roll(re, half, 1), im)
            grown_flat[layers + k, at] += jnp.where(later[p], zero, ends)
            grown_flat[2 * layers + k, at] += jnp.where(later[p], ends, zero)
        back = [product(window(p, k), back[p]) for p in range(slots)]
    total = []
    for i in range(2):
        total.append(sum(pltpu.roll(back[p][i], lax.rem(size - tops[p], size), 1) for p in range(slots)))
    pieces = sums.shape[0] // 2
    sums[:pieces] = total[0].T.reshape(pieces, *sums.shape[1:])
    sums[pieces:] = (-total[1]).T.reshape(pieces, *sums.shape[1:])
    copies = []

    def leave(source, target):
        copies.append(pltpu.make_async_copy(source, target, left_sem.at[len(copies)]))

    leave(sums, probe_sums)
    for g in range(groups):
        leave(grown.at[g, pl.ds(near, rows), core], keep_near.at[:, g])
        leave(grown.at[g, pl.ds(far, rows), core], keep_far.at[:, g])
        leave(grown.at[g, pl.ds(near, rows), other], send_near.at[:, g])
        leave(grown.at[g, pl.ds(far, rows), other], send_far.at[:, g])
    for copy in copies:
        copy.start()
    for copy in copies:
        copy.wait()


def summed(parts, first, last):
    total = parts[0, first:last]
    for q in range(1, parts.shape[0]):
        total = total + parts[q, first:last]
    return total


def probe_kernel(parts, many):
    total = summed(parts, 0, parts.shape[1])
    for q in range(many.shape[0]):
        many[q] = total


def share_kernel(info, kept, swapped, crossed, own, to_paired, to_crossed):
    layers = own.shape[1]
    odd = info[0] == 1
    for q in range(own.shape[0]):
        total = kept[q] + swapped[q] + crossed[q]
        before, after = total[layers : 2 * layers], total[2 * layers :]
        own[q] = total[:layers]
        to_paired[q] = jnp.where(odd, before, after)
        to_crossed[q] = jnp.where(odd, after, before)


def join_kernel(own, from_paired, from_crossed, parts, out):
    layers = own.shape[1]
    total = summed(parts, 0, parts.shape[1])
    total = total.reshape(out.shape[1] - layers, *out.shape[2:])
    for q in range(out.shape[0]):
        out[q, :layers] = own[q] + from_paired[q] + from_crossed[q]
        out[q, layers:] = total


def finish_kernel(shares, object_out, probe_out):
    layers, half = object_out.shape[1], object_out.shape[3]
    total = summed(shares, 0, layers)
    object_out[0] = total[:, :, :half]
    object_out[1] = total[:, :, half:]
    for q in range(shares.shape[0]):
        probe_out[q] = shares[q, layers:].reshape(probe_out.shape[1:])


def exchanged(array, axes):
    return lax.all_to_all(array, axes, 0, 0, tiled=True)


def local(object_slices, probe, intensities, row_offsets, column_starts, slice_shifts, counts):
    own = jnp.swapaxes(object_slices, 2, 3)
    layers, width, band = own.shape[1:]
    size = probe.shape[1]
    slots = row_offsets.shape[2]
    angles = lax.axis_size(ANGLE)
    plane = angles // 2
    rows = plane // 2
    scans = lax.axis_size(SCAN)
    pairs = [(i, i ^ 1) for i in range(scans)]
    others = [(i, i + 1 if i % 2 else i - 1) for i in range(1, scans - 1)]
    odd = lax.axis_index("xh").astype(jnp.int32)[None]
    swap = [(0, 1), (1, 0)]
    core = lax.axis_index("c")
    tile = (layers, width, 2 * band)
    groups = 3 * layers
    info = jnp.concatenate(
        [
            core.astype(jnp.int32)[None],
            lax.axis_index("xl").astype(jnp.int32)[None],
            row_offsets.reshape(slots),
            column_starts.reshape(slots),
            slice_shifts.reshape(layers),
            counts.reshape(1),
        ]
    )

    packed, packed_many = pl.pallas_call(
        pack_kernel,
        out_shape=(
            jax.ShapeDtypeStruct(tile, jnp.float32),
            jax.ShapeDtypeStruct((plane, *tile), jnp.float32),
        ),
        in_specs=[VMEM],
        out_specs=(VMEM, VMEM),
        compiler_params=SMALL,
    )(own)
    own_mine = exchanged(packed_many, PLANE)
    paired = lax.ppermute(packed, SCAN, pairs)
    crossed = lax.ppermute(packed, SCAN, others)
    rim_many = pl.pallas_call(
        repeat_kernel,
        out_shape=jax.ShapeDtypeStruct((plane, 2 * layers, *tile[1:]), jnp.float32),
        in_specs=[SMEM] + [VMEM] * 2 + [ANY],
        out_specs=VMEM,
        compiler_params=SMALL,
    )(odd, paired, crossed, own_mine)
    own_theirs = lax.ppermute(own_mine, "c", swap)
    rim_mine = exchanged(rim_many, PLANE)
    rim_theirs = lax.ppermute(rim_mine, "c", swap)

    share = jax.ShapeDtypeStruct((rows, groups, width, size), jnp.float32)
    depth = lax.axis_size("z")
    piece = jax.ShapeDtypeStruct((rows, 2 * size // rows, size), jnp.float32)
    table = jnp.asarray(tables(size))
    keep_near, keep_far, send_near, send_far, probe_sums = pl.pallas_call(
        gradient_kernel,
        out_shape=(share, share, *[pltpu.HBM(x.shape, x.dtype) for x in (share, share, piece)]),
        in_specs=[SMEM] + [HBM] * 3 + [ANY] * 4,
        out_specs=[HBM] * 5,
        scratch_shapes=[
            pltpu.VMEM((groups, plane, 2, width, size), jnp.float32),
            pltpu.VMEM((groups, plane, 2, width, size), jnp.float32),
            pltpu.VMEM(piece.shape, jnp.float32),
            pltpu.VMEM(table.shape, jnp.bfloat16),
            pltpu.VMEM(probe.shape, jnp.float32),
            pltpu.VMEM((slots, size, size), jnp.float32),
            pltpu.SemaphoreType.DMA((2 * groups + 3,)),
            pltpu.SemaphoreType.DMA((4 * groups + 1,)),
        ],
        compiler_params=pltpu.CompilerParams(vmem_limit_bytes=32 * 1024 * 1024),
    )(info, table, probe, intensities[0, 0], own_mine, own_theirs, rim_mine, rim_theirs)

    def probe_total(parts, count, cost=None):
        return pl.pallas_call(
            probe_kernel,
            out_shape=jax.ShapeDtypeStruct((count, *piece.shape[1:]), jnp.float32),
            in_specs=[VMEM],
            out_specs=VMEM,
            compiler_params=SMALL,
            cost_estimate=cost,
        )(parts)

    parts = exchanged(probe_sums, "y")
    part_far = keep_far + lax.ppermute(send_far, "c", swap)
    swapped = lax.ppermute(send_near, "c", swap)
    crossed = lax.ppermute(part_far, "xl", swap)
    parts = probe_total(parts, depth)
    parts, crossed, swapped = lax.optimization_barrier((parts, crossed, swapped))
    parts = exchanged(parts, "z")
    band_share = jax.ShapeDtypeStruct((rows, *tile), jnp.float32)
    own_share, to_paired, to_crossed = pl.pallas_call(
        share_kernel,
        out_shape=(band_share, band_share, band_share),
        in_specs=[SMEM] + [VMEM] * 3,
        out_specs=[VMEM] * 3,
        compiler_params=SMALL,
    )(odd, keep_near, swapped, crossed)
    parts = exchanged(probe_total(parts, lax.axis_size(ROW)), ROW)
    from_paired = lax.ppermute(to_paired, SCAN, pairs)
    from_crossed = lax.ppermute(to_crossed, SCAN, others)
    extra = piece.shape[1] // width
    joined = pl.pallas_call(
        join_kernel,
        out_shape=jax.ShapeDtypeStruct((rows, layers + extra, width, size), jnp.float32),
        in_specs=[VMEM] * 4,
        out_specs=VMEM,
        compiler_params=SMALL,
    )(own_share, from_paired, from_crossed, parts)
    object_gradient, probe_gradient = pl.pallas_call(
        finish_kernel,
        out_shape=(jax.ShapeDtypeStruct(own.shape, jnp.float32), piece),
        in_specs=[VMEM],
        out_specs=[VMEM] * 2,
        compiler_params=SMALL,
    )(exchanged(joined, "y"))
    return (jnp.swapaxes(object_gradient, 2, 3), probe_gradient.reshape(probe.shape))


def solution(mesh):
    devices = mesh.devices.reshape(2, 8, 2, 16, 2)
    fine = Mesh(devices, ("xl", "y", "c", "z", "xh"))
    return jax.shard_map(
        local,
        mesh=fine,
        in_specs=(
            P(None, None, SCAN, ANGLE),
            P(),
            P(ANGLE, SCAN, None, None, None),
            P(ANGLE, SCAN, None),
            P(ANGLE, SCAN, None),
            P(ANGLE, None),
            P(ANGLE, SCAN),
        ),
        out_specs=(P(None, None, SCAN, ANGLE), P()),
        check_vma=False,
    )
```

```python
import jax
import jax.numpy as jnp
import numpy as np
from jax import lax
from jax.experimental import pallas as pl
from jax.experimental.pallas import tpu as pltpu
from jax.sharding import Mesh
from jax.sharding import PartitionSpec as P

PLANE = ("xl", "y")
ANGLE = ("xl", "y", "c")
SCAN = ("z", "xh")
ROW = ("c", "xh")
ANY = pl.BlockSpec(memory_space=pl.ANY)
VMEM = pl.BlockSpec(memory_space=pltpu.VMEM)
SMEM = pl.BlockSpec(memory_space=pltpu.SMEM)
HBM = pl.BlockSpec(memory_space=pltpu.HBM)
SMALL = pltpu.CompilerParams(vmem_limit_bytes=8 * 1024 * 1024)


def tables(size):
    index = np.arange(size)
    centred = ((index + size // 2) % size - size // 2).astype(np.float64)
    dft = np.exp(-2j * np.pi * (np.outer(index, index) % size) / size) / np.sqrt(size)
    step = dft.conj() @ (np.exp(8j * np.pi * centred * centred / size**2)[:, None] * dft)
    whole = np.stack([np.stack([m.real, m.imag]) for m in (0.5 * (step + step.T), dft)]).astype(np.float32)
    high = whole.astype(jnp.bfloat16)
    low = (whole - high.astype(np.float32)).astype(jnp.bfloat16)
    return np.stack([high, low], axis=1)


def sides(table):
    left, right = [], []
    for part in (0, 1, 0):
        re, im = table[part, 0], table[part, 1]
        left.append(jnp.concatenate([jnp.concatenate([re, -im], axis=1), jnp.concatenate([im, re], axis=1)], axis=0))
        right.append(jnp.concatenate([jnp.concatenate([re, im], axis=1), jnp.concatenate([-im, re], axis=1)], axis=0))
    return jnp.concatenate(left, axis=1), jnp.concatenate(right, axis=0)


def parts(x, axis):
    high = x.astype(jnp.bfloat16)
    low = (x - high.astype(jnp.float32)).astype(jnp.bfloat16)
    return jnp.concatenate([high, high, low], axis=axis)


def two_sided(values, left, right):
    n = len(values)
    size = values[0][0].shape[0]
    stack = jnp.concatenate(
        [jnp.concatenate([v[i] for v in values], axis=1) for i in range(2)], axis=0
    )
    y = jnp.dot(left, parts(stack, 0), preferred_element_type=jnp.float32)
    rows = jnp.concatenate(
        [
            jnp.concatenate([y[i * size : (i + 1) * size, p * size : (p + 1) * size] for i in range(2)], axis=1)
            for p in range(n)
        ],
        axis=0,
    )
    z = jnp.dot(parts(rows, 1), right, preferred_element_type=jnp.float32)
    return [(z[p * size : (p + 1) * size, :size], z[p * size : (p + 1) * size, size:]) for p in range(n)]


def product(a, b):
    return (a[0] * b[0] - a[1] * b[1], a[0] * b[1] + a[1] * b[0])


def pack_kernel(own, out, many):
    tile = jnp.concatenate([own[0], own[1]], axis=2)
    out[...] = tile
    for q in range(many.shape[0]):
        many[q] = tile


def repeat_kernel(info, paired, crossed, unused, many):
    layers = paired.shape[0]
    odd = info[0] == 1
    before = jnp.where(odd, paired[...], crossed[...])
    after = jnp.where(odd, crossed[...], paired[...])
    for q in range(many.shape[0]):
        many[q, :layers] = before
        many[q, layers:] = after


def gradient_kernel(
    info, table, probe, measured, own_mine, own_theirs, rim_mine, rim_theirs,
    keep, send, probe_sums,
    region, grown, sums, table_here, probe_here, measured_here, arrived, left_sem,
):
    slots, size = measured.shape[0], measured.shape[1]
    groups = region.shape[0]
    layers = groups // 3
    half = size // 2
    angles = 2 * keep.shape[0]
    core = info[0]
    other = 1 - core
    place = 1
    copies = []

    def fetch(source, target):
        copies.append(pltpu.make_async_copy(source, target, arrived.at[len(copies)]))

    fetch(table, table_here)
    fetch(probe, probe_here)
    fetch(measured, measured_here)
    for g in range(groups):
        mine, theirs, at = (own_mine, own_theirs, g) if g < layers else (rim_mine, rim_theirs, g - layers)
        fetch(mine.at[:, at], region.at[g, :, core])
        fetch(theirs.at[:, at], region.at[g, :, other])
    for copy in copies:
        copy.start()
    grown[...] = jnp.zeros_like(grown)
    for copy in copies:
        copy.wait()
    wave = (probe_here[0].T, probe_here[1].T)
    meas = [measured_here[p].T for p in range(slots)]
    step = sides(table_here[0])
    dft = sides(table_here[1])
    columns = region.shape[1] * region.shape[2] * region.shape[3]
    flat = region.reshape(groups, columns, size)
    grown_flat = grown.reshape(groups, columns, size)
    lane = lax.broadcasted_iota(jnp.int32, (size, size), 1)
    rim = lane < half
    folded = jnp.where(rim, lane, lane - half)
    tops = [info[place + p] for p in range(slots)]
    later = [folded < tops[p] for p in range(slots)]
    weights = [jnp.where(p < info[place + 2 * slots + layers], 4.0 * 0.5 / angles, 0.0) for p in range(slots)]
    starts = [
        [info[place + slots + p] + info[place + 2 * slots + k] for k in range(layers)] for p in range(slots)
    ]

    def window(p, k):
        at = pl.ds(starts[p][k], size)
        own = flat[k, at]
        ends = jnp.where(later[p], flat[2 * layers + k, at], flat[layers + k, at])
        return (
            jnp.where(rim, ends, pltpu.roll(own, half, 1)),
            jnp.where(rim, pltpu.roll(ends, half, 1), own),
        )

    waves = [[tuple(pltpu.roll(w, tops[p], 1) for w in wave) for p in range(slots)]]
    for k in range(layers):
        leaving = [product(waves[k][p], window(p, k)) for p in range(slots)]
        waves.append(two_sided(leaving, *(step if k + 1 < layers else dft)))
    back = []
    for p in range(slots):
        re, im = waves[layers][p]
        slope = weights[p] * (re * re + im * im - meas[p])
        back.append((slope * re, -(slope * im)))
    for k in range(layers - 1, -1, -1):
        back = two_sided(back, *(step if k + 1 < layers else dft))
        for p in range(slots):
            at = pl.ds(starts[p][k], size)
            re, im = product(waves[k][p], back[p])
            im = -im
            zero = jnp.zeros_like(re)
            ends = jnp.where(rim, re, pltpu.roll(im, half, 1))
            grown_flat[k, at] += jnp.where(rim, pltpu.roll(re, half, 1), im)
            grown_flat[layers + k, at] += jnp.where(later[p], zero, ends)
            grown_flat[2 * layers + k, at] += jnp.where(later[p], ends, zero)
        back = [product(window(p, k), back[p]) for p in range(slots)]
    total = []
    for i in range(2):
        total.append(sum(pltpu.roll(back[p][i], lax.rem(size - tops[p], size), 1) for p in range(slots)))
    pieces = sums.shape[0] // 2
    sums[:pieces] = total[0].T.reshape(pieces, *sums.shape[1:])
    sums[pieces:] = (-total[1]).T.reshape(pieces, *sums.shape[1:])
    copies = []

    def leave(source, target):
        copies.append(pltpu.make_async_copy(source, target, left_sem.at[len(copies)]))

    leave(sums, probe_sums)
    for g in range(groups):
        leave(grown.at[g, :, core], keep.at[:, g])
        leave(grown.at[g, :, other], send.at[:, g])
    for copy in copies:
        copy.start()
    for copy in copies:
        copy.wait()


def summed(parts, first, last):
    total = parts[0, first:last]
    for q in range(1, parts.shape[0]):
        total = total + parts[q, first:last]
    return total


def probe_kernel(parts, many):
    total = summed(parts, 0, parts.shape[1])
    for q in range(many.shape[0]):
        many[q] = total


def share_kernel(info, kept, swapped, own, to_paired, to_crossed):
    layers = own.shape[1]
    odd = info[0] == 1
    for q in range(own.shape[0]):
        total = kept[q] + swapped[q]
        before, after = total[layers : 2 * layers], total[2 * layers :]
        own[q] = total[:layers]
        to_paired[q] = jnp.where(odd, before, after)
        to_crossed[q] = jnp.where(odd, after, before)


def join_kernel(own, from_paired, from_crossed, parts, out):
    layers = own.shape[1]
    total = summed(parts, 0, parts.shape[1])
    total = total.reshape(out.shape[1] - layers, *out.shape[2:])
    for q in range(out.shape[0]):
        out[q, :layers] = own[q] + from_paired[q] + from_crossed[q]
        out[q, layers:] = total


def finish_kernel(shares, object_out, probe_out):
    layers, half = object_out.shape[1], object_out.shape[3]
    total = summed(shares, 0, layers)
    object_out[0] = total[:, :, :half]
    object_out[1] = total[:, :, half:]
    for q in range(shares.shape[0]):
        probe_out[q] = shares[q, layers:].reshape(probe_out.shape[1:])


def exchanged(array, axes):
    return lax.all_to_all(array, axes, 0, 0, tiled=True)


def local(object_slices, probe, intensities, row_offsets, column_starts, slice_shifts, counts):
    own = jnp.swapaxes(object_slices, 2, 3)
    layers, width, band = own.shape[1:]
    size = probe.shape[1]
    slots = row_offsets.shape[2]
    angles = lax.axis_size(ANGLE)
    plane = angles // 2
    scans = lax.axis_size(SCAN)
    pairs = [(i, i ^ 1) for i in range(scans)]
    others = [(i, i + 1 if i % 2 else i - 1) for i in range(1, scans - 1)]
    odd = lax.axis_index("xh").astype(jnp.int32)[None]
    swap = [(0, 1), (1, 0)]
    core = lax.axis_index("c")
    tile = (layers, width, 2 * band)
    groups = 3 * layers
    info = jnp.concatenate(
        [
            core.astype(jnp.int32)[None],
            row_offsets.reshape(slots),
            column_starts.reshape(slots),
            slice_shifts.reshape(layers),
            counts.reshape(1),
        ]
    )

    packed, packed_many = pl.pallas_call(
        pack_kernel,
        out_shape=(
            jax.ShapeDtypeStruct(tile, jnp.float32),
            jax.ShapeDtypeStruct((plane, *tile), jnp.float32),
        ),
        in_specs=[VMEM],
        out_specs=(VMEM, VMEM),
        compiler_params=SMALL,
    )(own)
    own_mine = exchanged(packed_many, PLANE)
    paired = lax.ppermute(packed, SCAN, pairs)
    crossed = lax.ppermute(packed, SCAN, others)
    rim_many = pl.pallas_call(
        repeat_kernel,
        out_shape=jax.ShapeDtypeStruct((plane, 2 * layers, *tile[1:]), jnp.float32),
        in_specs=[SMEM] + [VMEM] * 2 + [ANY],
        out_specs=VMEM,
        compiler_params=SMALL,
    )(odd, paired, crossed, own_mine)
    own_theirs = lax.ppermute(own_mine, "c", swap)
    rim_mine = exchanged(rim_many, PLANE)
    rim_theirs = lax.ppermute(rim_mine, "c", swap)

    share = jax.ShapeDtypeStruct((plane, groups, width, size), jnp.float32)
    depth = lax.axis_size("z")
    piece = jax.ShapeDtypeStruct((plane, 2 * size // plane, size), jnp.float32)
    table = jnp.asarray(tables(size))
    keep, send, probe_sums = pl.pallas_call(
        gradient_kernel,
        out_shape=(share, *[pltpu.HBM(x.shape, x.dtype) for x in (share, piece)]),
        in_specs=[SMEM] + [HBM] * 3 + [ANY] * 4,
        out_specs=[HBM] * 3,
        scratch_shapes=[
            pltpu.VMEM((groups, plane, 2, width, size), jnp.float32),
            pltpu.VMEM((groups, plane, 2, width, size), jnp.float32),
            pltpu.VMEM(piece.shape, jnp.float32),
            pltpu.VMEM(table.shape, jnp.bfloat16),
            pltpu.VMEM(probe.shape, jnp.float32),
            pltpu.VMEM((slots, size, size), jnp.float32),
            pltpu.SemaphoreType.DMA((2 * groups + 3,)),
            pltpu.SemaphoreType.DMA((2 * groups + 1,)),
        ],
        compiler_params=pltpu.CompilerParams(vmem_limit_bytes=32 * 1024 * 1024),
    )(info, *[pltpu.with_memory_space_constraint(x, pltpu.HBM) for x in (table, probe, intensities[0, 0])], own_mine, own_theirs, rim_mine, rim_theirs)

    def probe_total(parts, count):
        return pl.pallas_call(
            probe_kernel,
            out_shape=jax.ShapeDtypeStruct((count, *piece.shape[1:]), jnp.float32),
            in_specs=[VMEM],
            out_specs=VMEM,
            compiler_params=SMALL,
        )(parts)

    parts = exchanged(probe_sums, PLANE)
    swapped = lax.ppermute(send, "c", swap)
    parts = exchanged(probe_total(parts, depth), "z")
    band_share = jax.ShapeDtypeStruct((plane, *tile), jnp.float32)
    own_share, to_paired, to_crossed = pl.pallas_call(
        share_kernel,
        out_shape=(band_share, band_share, band_share),
        in_specs=[SMEM] + [VMEM] * 2,
        out_specs=[VMEM] * 3,
        compiler_params=SMALL,
    )(odd, keep, swapped)
    parts = exchanged(probe_total(parts, lax.axis_size(ROW)), ROW)
    from_paired = lax.ppermute(to_paired, SCAN, pairs)
    from_crossed = lax.ppermute(to_crossed, SCAN, others)
    extra = piece.shape[1] // width
    joined = pl.pallas_call(
        join_kernel,
        out_shape=jax.ShapeDtypeStruct((plane, layers + extra, width, size), jnp.float32),
        in_specs=[VMEM] * 4,
        out_specs=VMEM,
        compiler_params=SMALL,
    )(own_share, from_paired, from_crossed, parts)
    object_gradient, probe_gradient = pl.pallas_call(
        finish_kernel,
        out_shape=(jax.ShapeDtypeStruct(own.shape, jnp.float32), piece),
        in_specs=[VMEM],
        out_specs=[VMEM] * 2,
        compiler_params=SMALL,
    )(exchanged(joined, PLANE))
    return (jnp.swapaxes(object_gradient, 2, 3), probe_gradient.reshape(probe.shape))


def solution(mesh):
    devices = mesh.devices.reshape(2, 8, 2, 16, 2)
    fine = Mesh(devices, ("xl", "y", "c", "z", "xh"))
    return jax.shard_map(
        local,
        mesh=fine,
        in_specs=(
            P(None, None, SCAN, ANGLE),
            P(),
            P(ANGLE, SCAN, None, None, None),
            P(ANGLE, SCAN, None),
            P(ANGLE, SCAN, None),
            P(ANGLE, None),
            P(ANGLE, SCAN),
        ),
        out_specs=(P(None, None, SCAN, ANGLE), P()),
        check_vma=False,
    )
```

```python
import jax
import jax.numpy as jnp
import numpy as np
from jax import lax
from jax.experimental import pallas as pl
from jax.experimental.pallas import tpu as pltpu
from jax.sharding import Mesh
from jax.sharding import PartitionSpec as P

PLANE = ("xl", "y")
ANGLE = ("xl", "y", "c")
SCAN = ("z", "xh")
ROW = ("c", "xh")
ANY = pl.BlockSpec(memory_space=pl.ANY)
VMEM = pl.BlockSpec(memory_space=pltpu.VMEM)
SMEM = pl.BlockSpec(memory_space=pltpu.SMEM)
HBM = pl.BlockSpec(memory_space=pltpu.HBM)
SMALL = pltpu.CompilerParams(vmem_limit_bytes=8 * 1024 * 1024)


def tables(size):
    index = np.arange(size)
    centred = ((index + size // 2) % size - size // 2).astype(np.float64)
    dft = np.exp(-2j * np.pi * (np.outer(index, index) % size) / size) / np.sqrt(size)
    step = dft.conj() @ (np.exp(8j * np.pi * centred * centred / size**2)[:, None] * dft)
    whole = np.stack([np.stack([m.real, m.imag]) for m in (0.5 * (step + step.T), dft)]).astype(np.float32)
    high = whole.astype(jnp.bfloat16)
    low = (whole - high.astype(np.float32)).astype(jnp.bfloat16)
    return np.stack([high, low], axis=1)


def sides(table):
    left, right = [], []
    for part in (0, 1, 0):
        re, im = table[part, 0], table[part, 1]
        left.append(jnp.concatenate([jnp.concatenate([re, -im], axis=1), jnp.concatenate([im, re], axis=1)], axis=0))
        right.append(jnp.concatenate([jnp.concatenate([re, im], axis=1), jnp.concatenate([-im, re], axis=1)], axis=0))
    return jnp.concatenate(left, axis=1), jnp.concatenate(right, axis=0)


def parts(x, axis):
    high = x.astype(jnp.bfloat16)
    low = (x - high.astype(jnp.float32)).astype(jnp.bfloat16)
    return jnp.concatenate([high, high, low], axis=axis)


def two_sided(values, left, right):
    n = len(values)
    size = values[0][0].shape[0]
    stack = jnp.concatenate(
        [jnp.concatenate([v[i] for v in values], axis=1) for i in range(2)], axis=0
    )
    y = jnp.dot(left, parts(stack, 0), preferred_element_type=jnp.float32)
    rows = jnp.concatenate(
        [
            jnp.concatenate([y[i * size : (i + 1) * size, p * size : (p + 1) * size] for i in range(2)], axis=1)
            for p in range(n)
        ],
        axis=0,
    )
    z = jnp.dot(parts(rows, 1), right, preferred_element_type=jnp.float32)
    return [(z[p * size : (p + 1) * size, :size], z[p * size : (p + 1) * size, size:]) for p in range(n)]


def product(a, b):
    return (a[0] * b[0] - a[1] * b[1], a[0] * b[1] + a[1] * b[0])


def pack_kernel(own, out, many):
    tile = jnp.concatenate([own[0], own[1]], axis=2)
    out[...] = tile
    for q in range(many.shape[0]):
        many[q] = tile


def repeat_kernel(info, paired, crossed, unused, many):
    layers = paired.shape[0]
    odd = info[0] == 1
    before = jnp.where(odd, paired[...], crossed[...])
    after = jnp.where(odd, crossed[...], paired[...])
    for q in range(many.shape[0]):
        many[q, :layers] = before
        many[q, layers:] = after


def gradient_kernel(
    info, table, probe, measured, own_mine, own_theirs, rim_mine, rim_theirs,
    keep, send, probe_sums,
    region, grown, sums, table_here, probe_here, measured_here, arrived, left_sem,
):
    slots, size = measured.shape[0], measured.shape[1]
    groups = region.shape[0]
    layers = groups // 3
    half = size // 2
    angles = 2 * keep.shape[0]
    core = info[0]
    other = 1 - core
    place = 1
    copies = []

    def fetch(source, target):
        copies.append(pltpu.make_async_copy(source, target, arrived.at[len(copies)]))

    fetch(table, table_here)
    fetch(probe, probe_here)
    fetch(measured, measured_here)
    for g in range(groups):
        mine, theirs, at = (own_mine, own_theirs, g) if g < layers else (rim_mine, rim_theirs, g - layers)
        fetch(mine.at[:, at], region.at[g, :, core])
        fetch(theirs.at[:, at], region.at[g, :, other])
    for copy in copies:
        copy.start()
    grown[...] = jnp.zeros_like(grown)
    for copy in copies:
        copy.wait()
    wave = (probe_here[0].T, probe_here[1].T)
    meas = [measured_here[p].T for p in range(slots)]
    step = sides(table_here[0])
    dft = sides(table_here[1])
    columns = region.shape[1] * region.shape[2] * region.shape[3]
    flat = region.reshape(groups, columns, size)
    grown_flat = grown.reshape(groups, columns, size)
    lane = lax.broadcasted_iota(jnp.int32, (size, size), 1)
    rim = lane < half
    folded = jnp.where(rim, lane, lane - half)
    tops = [info[place + p] for p in range(slots)]
    later = [folded < tops[p] for p in range(slots)]
    weights = [jnp.where(p < info[place + 2 * slots + layers], 4.0 * 0.5 / angles, 0.0) for p in range(slots)]
    starts = [
        [info[place + slots + p] + info[place + 2 * slots + k] for k in range(layers)] for p in range(slots)
    ]

    def window(p, k):
        at = pl.ds(starts[p][k], size)
        own = flat[k, at]
        ends = jnp.where(later[p], flat[2 * layers + k, at], flat[layers + k, at])
        return (
            jnp.where(rim, ends, pltpu.roll(own, half, 1)),
            jnp.where(rim, pltpu.roll(ends, half, 1), own),
        )

    waves = [[tuple(pltpu.roll(w, tops[p], 1) for w in wave) for p in range(slots)]]
    for k in range(layers):
        leaving = [product(waves[k][p], window(p, k)) for p in range(slots)]
        waves.append(two_sided(leaving, *(step if k + 1 < layers else dft)))
    back = []
    for p in range(slots):
        re, im = waves[layers][p]
        slope = weights[p] * (re * re + im * im - meas[p])
        back.append((slope * re, -(slope * im)))
    for k in range(layers - 1, -1, -1):
        back = two_sided(back, *(step if k + 1 < layers else dft))
        for p in range(slots):
            at = pl.ds(starts[p][k], size)
            re, im = product(waves[k][p], back[p])
            im = -im
            zero = jnp.zeros_like(re)
            ends = jnp.where(rim, re, pltpu.roll(im, half, 1))
            grown_flat[k, at] += jnp.where(rim, pltpu.roll(re, half, 1), im)
            grown_flat[layers + k, at] += jnp.where(later[p], zero, ends)
            grown_flat[2 * layers + k, at] += jnp.where(later[p], ends, zero)
        back = [product(window(p, k), back[p]) for p in range(slots)]
    total = []
    for i in range(2):
        total.append(sum(pltpu.roll(back[p][i], lax.rem(size - tops[p], size), 1) for p in range(slots)))
    pieces = sums.shape[0] // 2
    sums[:pieces] = total[0].T.reshape(pieces, *sums.shape[1:])
    sums[pieces:] = (-total[1]).T.reshape(pieces, *sums.shape[1:])
    copies = []

    def leave(source, target):
        copies.append(pltpu.make_async_copy(source, target, left_sem.at[len(copies)]))

    leave(sums, probe_sums)
    for g in range(groups):
        leave(grown.at[g, :, core], keep.at[:, g])
        leave(grown.at[g, :, other], send.at[:, g])
    for copy in copies:
        copy.start()
    for copy in copies:
        copy.wait()


def summed(parts, first, last):
    total = parts[0, first:last]
    for q in range(1, parts.shape[0]):
        total = total + parts[q, first:last]
    return total


def probe_kernel(parts, many):
    total = summed(parts, 0, parts.shape[1])
    for q in range(many.shape[0]):
        many[q] = total


def share_kernel(info, kept, swapped, own, to_paired, to_crossed):
    layers = own.shape[1]
    odd = info[0] == 1
    for q in range(own.shape[0]):
        total = kept[q] + swapped[q]
        before, after = total[layers : 2 * layers], total[2 * layers :]
        own[q] = total[:layers]
        to_paired[q] = jnp.where(odd, before, after)
        to_crossed[q] = jnp.where(odd, after, before)


def join_kernel(own, from_paired, from_crossed, parts, out):
    layers = own.shape[1]
    total = summed(parts, 0, parts.shape[1])
    total = total.reshape(out.shape[1] - layers, *out.shape[2:])
    for q in range(out.shape[0]):
        out[q, :layers] = own[q] + from_paired[q] + from_crossed[q]
        out[q, layers:] = total


def finish_kernel(shares, object_out, probe_out):
    layers, half = object_out.shape[1], object_out.shape[3]
    total = summed(shares, 0, layers)
    object_out[0] = total[:, :, :half]
    object_out[1] = total[:, :, half:]
    for q in range(shares.shape[0]):
        probe_out[q] = shares[q, layers:].reshape(probe_out.shape[1:])


def exchanged(array, axes):
    return lax.all_to_all(array, axes, 0, 0, tiled=True)


def local(object_slices, probe, intensities, row_offsets, column_starts, slice_shifts, counts):
    own = jnp.swapaxes(object_slices, 2, 3)
    layers, width, band = own.shape[1:]
    size = probe.shape[1]
    slots = row_offsets.shape[2]
    angles = lax.axis_size(ANGLE)
    plane = angles // 2
    scans = lax.axis_size(SCAN)
    pairs = [(i, i ^ 1) for i in range(scans)]
    others = [(i, i + 1 if i % 2 else i - 1) for i in range(1, scans - 1)]
    odd = lax.axis_index("xh").astype(jnp.int32)[None]
    swap = [(0, 1), (1, 0)]
    core = lax.axis_index("c")
    tile = (layers, width, 2 * band)
    groups = 3 * layers
    info = jnp.concatenate(
        [
            core.astype(jnp.int32)[None],
            row_offsets.reshape(slots),
            column_starts.reshape(slots),
            slice_shifts.reshape(layers),
            counts.reshape(1),
        ]
    )

    packed, packed_many = pl.pallas_call(
        pack_kernel,
        out_shape=(
            jax.ShapeDtypeStruct(tile, jnp.float32),
            jax.ShapeDtypeStruct((plane, *tile), jnp.float32),
        ),
        in_specs=[VMEM],
        out_specs=(VMEM, VMEM),
        compiler_params=SMALL,
    )(own)
    own_mine = exchanged(packed_many, PLANE)
    paired = lax.ppermute(packed, SCAN, pairs)
    crossed = lax.ppermute(packed, SCAN, others)
    rim_many = pl.pallas_call(
        repeat_kernel,
        out_shape=jax.ShapeDtypeStruct((plane, 2 * layers, *tile[1:]), jnp.float32),
        in_specs=[SMEM] + [VMEM] * 2 + [ANY],
        out_specs=VMEM,
        compiler_params=SMALL,
    )(odd, paired, crossed, own_mine)
    own_theirs = lax.ppermute(own_mine, "c", swap)
    rim_mine = exchanged(rim_many, PLANE)
    rim_mine, own_theirs = lax.optimization_barrier((rim_mine, own_theirs))
    rim_theirs = lax.ppermute(rim_mine, "c", swap)

    share = jax.ShapeDtypeStruct((plane, groups, width, size), jnp.float32)
    depth = lax.axis_size("z")
    piece = jax.ShapeDtypeStruct((plane, 2 * size // plane, size), jnp.float32)
    table = jnp.asarray(tables(size))
    keep, send, probe_sums = pl.pallas_call(
        gradient_kernel,
        out_shape=(share, *[pltpu.HBM(x.shape, x.dtype) for x in (share, piece)]),
        in_specs=[SMEM] + [HBM] * 3 + [ANY] * 4,
        out_specs=[HBM] * 3,
        scratch_shapes=[
            pltpu.VMEM((groups, plane, 2, width, size), jnp.float32),
            pltpu.VMEM((groups, plane, 2, width, size), jnp.float32),
            pltpu.VMEM(piece.shape, jnp.float32),
            pltpu.VMEM(table.shape, jnp.bfloat16),
            pltpu.VMEM(probe.shape, jnp.float32),
            pltpu.VMEM((slots, size, size), jnp.float32),
            pltpu.SemaphoreType.DMA((2 * groups + 3,)),
            pltpu.SemaphoreType.DMA((2 * groups + 1,)),
        ],
        compiler_params=pltpu.CompilerParams(vmem_limit_bytes=32 * 1024 * 1024),
    )(info, *[pltpu.with_memory_space_constraint(x, pltpu.HBM) for x in (table, probe, intensities[0, 0])], own_mine, own_theirs, rim_mine, rim_theirs)

    def probe_total(parts, count):
        return pl.pallas_call(
            probe_kernel,
            out_shape=jax.ShapeDtypeStruct((count, *piece.shape[1:]), jnp.float32),
            in_specs=[VMEM],
            out_specs=VMEM,
            compiler_params=SMALL,
        )(parts)

    parts = exchanged(probe_sums, PLANE)
    swapped = lax.ppermute(send, "c", swap)
    parts = exchanged(probe_total(parts, depth), "z")
    band_share = jax.ShapeDtypeStruct((plane, *tile), jnp.float32)
    own_share, to_paired, to_crossed = pl.pallas_call(
        share_kernel,
        out_shape=(band_share, band_share, band_share),
        in_specs=[SMEM] + [VMEM] * 2,
        out_specs=[VMEM] * 3,
        compiler_params=SMALL,
    )(odd, keep, swapped)
    parts = exchanged(probe_total(parts, lax.axis_size(ROW)), ROW)
    from_paired = lax.ppermute(to_paired, SCAN, pairs)
    from_crossed = lax.ppermute(to_crossed, SCAN, others)
    extra = piece.shape[1] // width
    joined = pl.pallas_call(
        join_kernel,
        out_shape=jax.ShapeDtypeStruct((plane, layers + extra, width, size), jnp.float32),
        in_specs=[VMEM] * 4,
        out_specs=VMEM,
        compiler_params=SMALL,
    )(own_share, from_paired, from_crossed, parts)
    object_gradient, probe_gradient = pl.pallas_call(
        finish_kernel,
        out_shape=(jax.ShapeDtypeStruct(own.shape, jnp.float32), piece),
        in_specs=[VMEM],
        out_specs=[VMEM] * 2,
        compiler_params=SMALL,
    )(exchanged(joined, PLANE))
    return (jnp.swapaxes(object_gradient, 2, 3), probe_gradient.reshape(probe.shape))


def solution(mesh):
    devices = mesh.devices.reshape(2, 8, 2, 16, 2)
    fine = Mesh(devices, ("xl", "y", "c", "z", "xh"))
    return jax.shard_map(
        local,
        mesh=fine,
        in_specs=(
            P(None, None, SCAN, ANGLE),
            P(),
            P(ANGLE, SCAN, None, None, None),
            P(ANGLE, SCAN, None),
            P(ANGLE, SCAN, None),
            P(ANGLE, None),
            P(ANGLE, SCAN),
        ),
        out_specs=(P(None, None, SCAN, ANGLE), P()),
        check_vma=False,
    )
```
